512 devices in a mesh: row: 8 (over y, z_hi), col: 64 (over z_lo, x, core).
Axes of the slice: x: 4, y: 4, z: 16 (z_hi: 2, z_lo: 8; z = z_hi * 8 + z_lo), core: 2. Of those that a mesh axis runs over, the one named last changes fastest.
Arguments:
- side_a: float32 [64, 8192], P('row', 'col'), may hold values from -6 to 6
- side_b: float32 [2048, 8192], P('col', 'row'), may hold values from -6 to 6
- pair_grad: float32 [64, 2048, 128], P('row', 'col'), may hold values from -6 to 6
- out_weight: float32 [1024, 128], replicated, may hold values from -0.1875 to 0.1875
Outputs:
- grad_a: float32 [64, 8192], P('row', 'col')
- grad_b: float32 [2048, 8192], P('col', 'row')
- grad_weight: float32 [1024, 128], replicated
- grad_bias: float32 [128], replicated
The draws below stay inside these ranges and needn't reach their ends.
All inputs are finite; a program needn't handle non-finite values.
Results may differ from the reference program's by a relative error of at most 0.00013.
Values sent between devices are 32-bit elements; how exact they have to be, the bound alone decides.
A program may use at most 64 MiB of HBM per device.

```python
import math
import jax
import jax.numpy as jnp
from jax import lax

S = 256
C = 32
P_SIZE = 128
LI = 64
LJ = 2048


def steps_of(stream_key, dims, cuts, smallest, top_value):
    loudness = 1.0
    for axis_at, blocks in cuts:
        draws = jax.random.uniform(jax.random.fold_in(jax.random.fold_in(stream_key, 6), axis_at), (blocks,), jnp.float32, smallest / len(cuts), top_value / len(cuts))
        loudness = loudness * jnp.repeat(jnp.exp(draws), dims[axis_at] // blocks).reshape((-1,) + (1,) * (len(dims) - 1 - axis_at))
    return loudness


def normal_values(rng, dims, width, bound, shards=(), dtype=jnp.bfloat16):
    gain = steps_of(rng, dims, shards, -0.22, 0.18) if shards else 1.0
    result = jax.random.normal(rng, dims, jnp.float32) * width * gain
    return jnp.minimum(jnp.maximum(result, -bound), bound).astype(dtype)


def setup_inputs(seed: int = 0) -> dict:
    key_list = jax.random.split(jax.random.key(seed), 5)
    side_a = normal_values(key_list[0], (LI, S * C), 1.0, 6.0, ((0, 8), (1, 64)), jnp.float32)
    side_b = normal_values(key_list[1], (LJ, S * C), 1.0, 6.0, ((0, 64), (1, 8)), jnp.float32)
    pair_grad = normal_values(key_list[2], (LI, LJ, P_SIZE), 1.0, 6.0, ((0, 8), (1, 64)), jnp.float32)
    out_weight = normal_values(key_list[3], (C * C, P_SIZE), (C * C) ** -0.5, 0.1875, (), jnp.float32)
    return {"side_a": side_a, "side_b": side_b, "pair_grad": pair_grad, "out_weight": out_weight}


def tile_terms(left_piece, right_flat, pair_piece, out_weight):
    high = lax.Precision.HIGHEST
    rows = left_piece.shape[0]
    cols = right_flat.shape[1] // C
    left_flat = jnp.transpose(left_piece, (0, 2, 1)).reshape(rows * C, S)
    flat_pair = pair_piece.reshape(rows * cols, P_SIZE)
    grad_outer = jnp.dot(flat_pair, out_weight.T, precision=high)
    grad_tile = jnp.transpose(grad_outer.reshape(rows, cols, C, C), (0, 2, 1, 3)).reshape(rows * C, cols * C)
    left_grad = jnp.dot(grad_tile, right_flat.T, precision=high) / S
    left_grad = jnp.transpose(left_grad.reshape(rows, C, S), (0, 2, 1))
    right_grad = jnp.dot(left_flat.T, grad_tile, precision=high) / S
    outer = jnp.dot(left_flat, right_flat, precision=high) / S
    outer = jnp.transpose(outer.reshape(rows, C, cols, C), (0, 2, 1, 3)).reshape(rows * cols, C * C)
    weight_part = jnp.dot(outer.T, flat_pair, precision=high)
    return left_grad, right_grad, weight_part


def reference(side_a, side_b, pair_grad, out_weight):
    left = side_a.reshape(LI, S, C)
    right = side_b.reshape(LJ, S, C)
    right_flat = jnp.transpose(right, (1, 0, 2)).reshape(S, LJ * C)
    block = math.gcd(LI, 8)
    left_blocks = left.reshape(LI // block, block, S, C)
    pair_blocks = pair_grad.reshape(LI // block, block, LJ, P_SIZE)

    def step(carry, pieces):
        right_total, weight_total = carry
        left_piece, pair_piece = pieces
        left_grad, right_part, weight_part = tile_terms(left_piece, right_flat, pair_piece, out_weight)
        return (right_total + right_part, weight_total + weight_part), left_grad

    start = (jnp.zeros((S, LJ * C), jnp.float32), jnp.zeros((C * C, P_SIZE), jnp.float32))
    (right_total, weight_total), left_grads = lax.scan(step, start, (left_blocks, pair_blocks))
    grad_a = left_grads.reshape(LI, S * C)
    grad_b = jnp.transpose(right_total.reshape(S, LJ, C), (1, 0, 2)).reshape(LJ, S * C)
    grad_bias = jnp.sum(pair_grad, axis=(0, 1))
    return grad_a, grad_b, weight_total, grad_bias
```

```python
import jax
import jax.numpy as jnp
from jax import lax
from jax.experimental import pallas as pl
from jax.experimental.pallas import tpu as pltpu
from jax.sharding import PartitionSpec as P

S = 256
C = 32
K = 128
CHUNKS = 4
JC = 32 // CHUNKS
MESH = pl.DeviceIdType.MESH
F32 = jnp.float32
BF16 = jnp.bfloat16

Y_OWN = 0
TWIN = Y_OWN + 3
FWD = TWIN + CHUNKS
A_ONE = FWD + 3 * CHUNKS
A_X = A_ONE + 8
A_CORE = A_X + 3
GA_CORE = A_CORE + 1
GA_X = GA_CORE + 1
GA_Z = GA_X + 3
W_CORE = GA_Z + 8
B_CORE = W_CORE + 1
W_XY = B_CORE + 1
W_Z1 = W_XY + 16
W_Z2 = W_Z1 + 3
W_AG = W_Z2 + 3
W_END = W_AG + 16
N_SEM = W_END + 1

CONTRACT_LANES = (((1,), (1,)), ((), ()))


def high(x):
    return x.astype(BF16).astype(F32)


def kernel(
    a_ref,
    b_ref,
    pg_ref,
    w_ref,
    ga_out,
    gb_out,
    gw_out,
    bias_out,
    g_all,
    a_all,
    ga_all,
    ga_r1,
    ga_r2,
    ga_s,
    ga_r3,
    gw_part,
    gw_r1,
    gw_s,
    gw_r2,
    gw_z1,
    gw_z2,
    bias_own,
    bias_r1,
    t_h,
    t_l,
    u_h,
    u_l,
    wt,
    bs,
    bjs,
    bp,
    bt,
    at1,
    at2,
    ap,
    gi,
    acc_a,
    acc_w,
    send_sem,
    recv_sem,
):
    r = lax.axis_index("row")
    q = lax.axis_index("col")
    y = r // 2
    zh = r % 2
    zl = q // 8
    x = (q // 2) % 4
    core = q % 2
    z = zh * 8 + zl
    place = core * 4 + x
    xy = x * 4 + y

    def dev(y_, z_, x_, core_):
        return (y_ * 2 + z_ // 8, (z_ % 8) * 8 + x_ * 2 + core_)

    def rcopy(src, dst, number, device, arrives=None):
        return pltpu.make_async_remote_copy(
            src_ref=src,
            dst_ref=dst,
            send_sem=send_sem.at[number],
            recv_sem=recv_sem.at[number if arrives is None else arrives],
            device_id=device,
            device_id_type=MESH,
        )

    sibling = dev(y, z, x, 1 - core)
    twin = dev(y, (z + 8) % 16, x, core)
    y_peers = [dev((y + d) % 4, z, x, core) for d in (1, 2, 3)]
    x_peers = [dev(y, z, (x + d) % 4, core) for d in (1, 2, 3)]
    xy_steps = [(dx, dy) for dx in range(4) for dy in range(4) if (dx, dy) != (0, 0)]
    xy_peers = [dev((y + dy) % 4, z, (x + dx) % 4, core) for dx, dy in xy_steps]
    z_near = [dev(y, (z // 4) * 4 + (z + d) % 4, x, core) for d in (1, 2, 3)]
    z_far = [dev(y, (z + 4 * d) % 16, x, core) for d in (1, 2, 3)]
    out_a = [(zl, ((zl + d) % 8) * 8 + x * 2 + core) for d in range(8)]
    in_a = [((r + d) % 8, r * 8 + x * 2 + core) for d in range(8)]
    at_home = zl == r

    barrier = pltpu.get_barrier_semaphore()

    def greet(device):
        pl.semaphore_signal(barrier, inc=1, device_id=device, device_id_type=MESH)

    for device in out_a[1:] + in_a[1:] + z_far + z_near + xy_peers + [sibling]:
        greet(device)

    @pl.when(jnp.logical_not(at_home))
    def _():
        greet(out_a[0])
        greet(in_a[0])

    bias = jnp.zeros((8, K), F32)
    for j in range(32):
        block = pg_ref[pl.ds(j, 8, stride=32), :]
        g_all[r, j] = block
        bias = bias + block
    bias_own[...] = bias

    @pl.when(at_home)
    def _():
        a_all[place, r] = a_ref[...]

    fixed = 14 + 3 + 3 + 15 + 1
    pl.semaphore_wait(barrier, fixed + jnp.where(at_home, 0, 2))

    def chunk(m):
        return pl.ds(m * JC, JC)

    started = []

    def start(copy):
        copy.start()
        started.append(copy)
        return copy

    twin_copies = [
        rcopy(g_all.at[r, chunk(m)], g_all.at[r, chunk(m)], TWIN + m, twin) for m in range(CHUNKS)
    ]
    start(twin_copies[0])
    a_copies = [
        rcopy(a_ref, a_all.at[place, r], A_ONE + d, out_a[d], A_ONE + r) for d in range(8)
    ]
    a_waits = [
        rcopy(a_ref, a_all.at[place, r], A_ONE + d, out_a[d], A_ONE + (r + d) % 8)
        for d in range(8)
    ]

    @pl.when(jnp.logical_not(at_home))
    def _():
        a_copies[0].start()

    for d in range(1, 8):
        start(a_copies[d])
    for m in range(1, CHUNKS):
        start(twin_copies[m])
    own_copies = [start(rcopy(g_all.at[r], g_all.at[r], Y_OWN + n, y_peers[n])) for n in range(3)]

    wt[96:128, :] = jnp.zeros((32, 4096), BF16)

    def prep_w(c, _):
        w = w_ref[pl.ds(pl.multiple_of(c * 32, 32), 32), :]
        lanes = pl.ds(pl.multiple_of(c * 128, 128), 128)
        h = w.astype(BF16)
        l = (w - h.astype(F32)).astype(BF16)
        wt[0:32, lanes] = h
        wt[32:64, lanes] = l
        wt[64:96, lanes] = h
        return 0

    lax.fori_loop(0, 32, prep_w, 0)

    for s in range(32):
        v = b_ref[:, s * 32 : (s + 1) * 32]
        h = high(v)
        bs[s * 32 : (s + 1) * 32, :] = jnp.concatenate([h, h, v - h, jnp.zeros_like(v)], axis=1)
    for j in range(32):
        v = bs[pl.ds(j, 32, stride=32), :]
        bjs[j * 32 : (j + 1) * 32, :] = v
        bp[j * 32 : (j + 1) * 32, :] = v.astype(BF16)
    for n in range(8):
        bt[:, n * 128 : (n + 1) * 128] = bjs[n * 128 : (n + 1) * 128, :].T.astype(BF16)

    def make_t(m):
        def step(cp, _):
            v = jnp.dot(
                bp[m * JC * 32 : (m + 1) * JC * 32, :],
                wt[:, pl.ds(pl.multiple_of(cp * 256, 256), 256)],
                preferred_element_type=F32,
            )
            h = v.astype(BF16)
            l = (v - h.astype(F32)).astype(BF16)
            for cc in range(2):
                rows = pl.ds(pl.multiple_of(cp * 64 + cc * 32, 32), 32)
                for j in range(JC):
                    lanes = slice((m * JC + j) * 128, (m * JC + j + 1) * 128)
                    t_h[rows, lanes] = h[j * 32 : (j + 1) * 32, cc * 128 : (cc + 1) * 128]
                    t_l[rows, lanes] = l[j * 32 : (j + 1) * 32, cc * 128 : (cc + 1) * 128]
            return 0

        lax.fori_loop(0, 16, step, 0)

    forwards = {}

    def forward(m):
        twin_copies[m].wait_recv()
        for n in range(3):
            src = g_all.at[r + 1 - 2 * zh, chunk(m)]
            forwards[m, n] = start(rcopy(src, src, FWD + 3 * m + n, y_peers[n]))

    make_t(0)
    make_t(1)
    for d in range(1, 8):
        a_waits[d].wait_recv()

    @pl.when(jnp.logical_not(at_home))
    def _():
        a_waits[0].wait_recv()

    ax_copies = [
        start(rcopy(a_all.at[place], a_all.at[place], A_X + n, x_peers[n])) for n in range(3)
    ]
    forward(0)
    make_t(2)
    for copy in ax_copies:
        copy.wait_recv()
    half = a_all.at[pl.ds(core * 4, 4)]
    ac_copy = start(rcopy(half, half, A_CORE, sibling))
    forward(1)
    make_t(3)
    ac_copy.wait_recv()
    zeros = jnp.zeros((64, 128), F32)
    for core_ in range(2):
        for x_ in range(4):
            v = a_all[core_ * 4 + x_].reshape(64, 128)
            h = high(v)
            rows = slice((x_ * 2 + core_) * 128, (x_ * 2 + core_ + 1) * 128)
            at1[rows, :] = jnp.concatenate([h, h], axis=0).T
            at2[rows, :] = jnp.concatenate([v - h, zeros], axis=0).T
    for c in range(32):
        ap[c * 32 : (c + 1) * 32, 0:128] = at1[pl.ds(c, 32, stride=32), :].astype(BF16)
        ap[c * 32 : (c + 1) * 32, 128:256] = at2[pl.ds(c, 32, stride=32), :].astype(BF16)
    gi[192:256, :] = jnp.zeros((64, JC * 128), BF16)
    for copy in own_copies:
        copy.wait_recv()

    rows_m = JC * 32
    for m in range(CHUNKS):
        for n in range(3):
            forwards[m, n].wait_recv()
        for j in range(JC):
            v = g_all[:, m * JC + j].reshape(64, 128)
            h = v.astype(BF16)
            l = (v - h.astype(F32)).astype(BF16)
            gi[0:64, j * 128 : (j + 1) * 128] = h
            gi[64:128, j * 128 : (j + 1) * 128] = l
            gi[128:192, j * 128 : (j + 1) * 128] = h

        def make_u(n, _):
            v_rows = pl.ds(pl.multiple_of(n * 256, 256), 256)
            for jp in range(JC // 2):
                v = jnp.dot(
                    ap[v_rows, :], gi[:, jp * 256 : (jp + 1) * 256], preferred_element_type=F32
                )
                h = v.astype(BF16)
                l = (v - h.astype(F32)).astype(BF16)
                for jj in range(2):
                    rows = slice((m * JC + jp * 2 + jj) * 32, (m * JC + jp * 2 + jj + 1) * 32)
                    for c in range(8):
                        lanes = pl.ds(pl.multiple_of(n * 1024 + c * 128, 128), 128)
                        u_h[rows, lanes] = h[c * 32 : (c + 1) * 32, jj * 128 : (jj + 1) * 128]
                        u_l[rows, lanes] = l[c * 32 : (c + 1) * 32, jj * 128 : (jj + 1) * 128]
            return 0

        lax.fori_loop(0, 4, make_u, 0)

        def add_w(cp, _):
            lanes = pl.ds(pl.multiple_of(cp * 256, 256), 256)
            left = bt[32:96, m * rows_m : (m + 1) * rows_m]
            v = jnp.dot(
                left, u_h[m * rows_m : (m + 1) * rows_m, lanes], preferred_element_type=F32
            ) + jnp.dot(left, u_l[m * rows_m : (m + 1) * rows_m, lanes], preferred_element_type=F32)
            acc_w[:, lanes] = v if m == 0 else acc_w[:, lanes] + v
            return 0

        lax.fori_loop(0, 16, add_w, 0)
        if m + 2 < CHUNKS:
            forward(m + 2)

        def add_a(n, _):
            rows = pl.ds(pl.multiple_of(n * 256, 256), 256)
            lanes = slice(m * JC * 128, (m + 1) * JC * 128)
            v = lax.dot_general(
                t_h[rows, lanes], gi[0:128, :], CONTRACT_LANES, preferred_element_type=F32
            ) + lax.dot_general(
                t_l[rows, lanes], gi[0:128, :], CONTRACT_LANES, preferred_element_type=F32
            )
            acc_a[rows, :] = v if m == 0 else acc_a[rows, :] + v
            return 0

        lax.fori_loop(0, 4, add_a, 0)

    def fold_w(c, _):
        lanes = pl.ds(pl.multiple_of(c * 128, 128), 128)
        gw_part[pl.ds(pl.multiple_of(c * 32, 32), 32), :] = (
            acc_w[0:32, lanes] + acc_w[32:64, lanes]
        ) * (1.0 / S)
        return 0

    lax.fori_loop(0, 32, fold_w, 0)
    other = pl.ds(pl.multiple_of((1 - core) * 512, 512), 512)
    w_core = start(rcopy(gw_part.at[other], gw_r1, W_CORE, sibling))
    b_core = start(rcopy(bias_own, bias_r1, B_CORE, sibling))

    for core_ in range(2):
        for x_ in range(4):
            s0 = 4 * (x_ * 2 + core_)
            v = jnp.concatenate(
                [acc_a[pl.ds(s0 + s, 32, stride=32), :] for s in range(4)], axis=0
            ).T
            ga_all[core_, x_] = ((v[0:64] + v[64:128]) * (1.0 / S)).reshape(8, 8, 128)
    ga_core = start(rcopy(ga_all.at[1 - core], ga_r1, GA_CORE, sibling))

    w_core.wait_recv()
    b_core.wait_recv()
    bias = bias_own[...] + bias_r1[...]

    def add_core(n, _):
        rows = pl.ds(pl.multiple_of(n * 32, 32), 32)
        mine = pl.ds(pl.multiple_of(core * 512 + n * 32, 32), 32)
        gw_s[n, 0:32] = gw_part[mine, :] + gw_r1[rows, :]
        gw_s[n, 32:40] = bias
        return 0

    lax.fori_loop(0, 16, add_core, 0)
    gw_r2[xy] = gw_s[xy]
    w_xy = []
    for n, (dx, dy) in enumerate(xy_steps):
        to = ((x + dx) % 4) * 4 + (y + dy) % 4
        w_xy.append(start(rcopy(gw_s.at[to], gw_r2.at[xy], W_XY + n, xy_peers[n])))

    ga_core.wait_recv()
    for x_ in range(4):
        ga_r1[x_] = ga_r1[x_] + ga_all[core, x_]
    ga_r2[x] = ga_r1[x]
    ga_x = []
    for n, d in enumerate((1, 2, 3)):
        ga_x.append(start(rcopy(ga_r1.at[(x + d) % 4], ga_r2.at[x], GA_X + n, x_peers[n])))

    def add_b(m):
        rows = slice(m * rows_m, (m + 1) * rows_m)

        def step(n, v):
            lanes = pl.ds(pl.multiple_of(n * 1024, 1024), 1024)
            right = wt[0:64, lanes]
            return (
                v
                + lax.dot_general(u_h[rows, lanes], right, CONTRACT_LANES, preferred_element_type=F32)
                + lax.dot_general(u_l[rows, lanes], right, CONTRACT_LANES, preferred_element_type=F32)
            )

        v = lax.fori_loop(0, 4, step, jnp.zeros((rows_m, 64), F32))
        bjs[rows, 0:32] = (v[:, 0:32] + v[:, 32:64]) * (1.0 / S)

    add_b(0)
    for copy in w_xy:
        copy.wait_recv()
    v = gw_r2[0]
    for n in range(1, 16):
        v = v + gw_r2[n]
    gw_z1[z % 4] = v
    w_z1 = [
        start(rcopy(gw_z1.at[z % 4], gw_z1.at[z % 4], W_Z1 + n, z_near[n])) for n in range(3)
    ]
    for copy in ga_x:
        copy.wait_recv()
    ga_s[...] = (ga_r2[0] + ga_r2[1]) + (ga_r2[2] + ga_r2[3])
    ga_z = [
        rcopy(ga_s.at[(r + d) % 8], ga_r3.at[zl], GA_Z + d, in_a[d], GA_Z + zl) for d in range(8)
    ]
    ga_waits = [
        rcopy(ga_s.at[d], ga_r3.at[zl], GA_Z + d, in_a[d], GA_Z + (zl + d) % 8) for d in range(8)
    ]

    @pl.when(jnp.logical_not(at_home))
    def _():
        ga_z[0].start()

    @pl.when(at_home)
    def _():
        ga_r3[zl] = ga_s[r]

    for d in range(1, 8):
        start(ga_z[d])
    add_b(1)
    for copy in w_z1:
        copy.wait_recv()
    gw_z2[z // 4] = (gw_z1[0] + gw_z1[1]) + (gw_z1[2] + gw_z1[3])
    w_z2 = [
        start(rcopy(gw_z2.at[z // 4], gw_z2.at[z // 4], W_Z2 + n, z_far[n])) for n in range(3)
    ]
    add_b(2)
    add_b(3)
    for s in range(32):
        gb_out[:, s * 32 : (s + 1) * 32] = bjs[pl.ds(s, 32, stride=32), 0:32]
    for copy in w_z2:
        copy.wait_recv()
    v = (gw_z2[0] + gw_z2[1]) + (gw_z2[2] + gw_z2[3])
    mine = pl.ds(pl.multiple_of(core * 512 + xy * 32, 32), 32)
    gw_out[mine, :] = v[0:32]
    bias_out[...] = jnp.sum(v[32:40], axis=0, keepdims=True)
    w_ag = [
        start(rcopy(gw_out.at[mine], gw_out.at[mine], W_AG + n, xy_peers[n])) for n in range(15)
    ]
    for d in range(1, 8):
        ga_waits[d].wait_recv()

    @pl.when(jnp.logical_not(at_home))
    def _():
        ga_waits[0].wait_recv()

    v = ga_r3[0]
    for n in range(1, 8):
        v = v + ga_r3[n]
    ga_out[...] = v
    for copy in w_ag:
        copy.wait_recv()
    mine = gw_out.at[pl.ds(pl.multiple_of(core * 512, 512), 512)]
    w_end = start(rcopy(mine, mine, W_END, sibling))
    w_end.wait_recv()
    for copy in started:
        copy.wait_send()

    @pl.when(jnp.logical_not(at_home))
    def _():
        a_copies[0].wait_send()
        ga_z[0].wait_send()


def local(side_a, side_b, pair_grad, out_weight):
    vmem = pl.BlockSpec(memory_space=pltpu.VMEM)
    flat = pair_grad.reshape(256, K)
    ga, gb, gw, bias = pl.pallas_call(
        kernel,
        out_shape=(
            jax.ShapeDtypeStruct((8, 128), F32),
            jax.ShapeDtypeStruct((32, 1024), F32),
            jax.ShapeDtypeStruct((1024, 128), F32),
            jax.ShapeDtypeStruct((1, 128), F32),
        ),
        in_specs=[vmem] * 4,
        out_specs=(vmem,) * 4,
        scratch_shapes=[
            pltpu.VMEM((8, 32, 8, 128), F32),
            pltpu.VMEM((8, 8, 8, 128), F32),
            pltpu.VMEM((2, 4, 8, 8, 128), F32),
            pltpu.VMEM((4, 8, 8, 128), F32),
            pltpu.VMEM((4, 8, 8, 128), F32),
            pltpu.VMEM((8, 8, 128), F32),
            pltpu.VMEM((8, 8, 128), F32),
            pltpu.VMEM((1024, 128), F32),
            pltpu.VMEM((512, 128), F32),
            pltpu.VMEM((16, 40, 128), F32),
            pltpu.VMEM((16, 40, 128), F32),
            pltpu.VMEM((4, 40, 128), F32),
            pltpu.VMEM((4, 40, 128), F32),
            pltpu.VMEM((8, 128), F32),
            pltpu.VMEM((8, 128), F32),
            pltpu.VMEM((1024, 4096), BF16),
            pltpu.VMEM((1024, 4096), BF16),
            pltpu.VMEM((1024, 4096), BF16),
            pltpu.VMEM((1024, 4096), BF16),
            pltpu.VMEM((128, 4096), BF16),
            pltpu.VMEM((1024, 128), F32),
            pltpu.VMEM((1024, 128), F32),
            pltpu.VMEM((1024, 128), BF16),
            pltpu.VMEM((128, 1024), BF16),
            pltpu.VMEM((1024, 128), F32),
            pltpu.VMEM((1024, 128), F32),
            pltpu.VMEM((1024, 256), BF16),
            pltpu.VMEM((256, JC * 128), BF16),
            pltpu.VMEM((1024, 128), F32),
            pltpu.VMEM((64, 4096), F32),
            pltpu.SemaphoreType.DMA((N_SEM,)),
            pltpu.SemaphoreType.DMA((N_SEM,)),
        ],
        compiler_params=pltpu.CompilerParams(
            collective_id=0, has_side_effects=True, vmem_limit_bytes=60 * 1024 * 1024
        ),
    )(side_a, side_b, flat, out_weight)
    return ga, gb, gw, bias.reshape(K)


def solution(mesh):
    in_specs = (P("row", "col"), P("col", "row"), P("row", "col", None), P())
    out_specs = (P("row", "col"), P("col", "row"), P(), P())
    return jax.shard_map(local, mesh=mesh, in_specs=in_specs, out_specs=out_specs, check_vma=False)
```

```python
import jax
import jax.numpy as jnp
from jax import lax
from jax.experimental import pallas as pl
from jax.experimental.pallas import tpu as pltpu
from jax.sharding import PartitionSpec as P

S = 256
C = 32
K = 128
CHUNKS = 8
TC = 32 // CHUNKS
JC = 8
MESH = pl.DeviceIdType.MESH
F32 = jnp.float32
BF16 = jnp.bfloat16

Y_OWN = 0
TWIN = Y_OWN + 3
FWD = TWIN + CHUNKS
A_ONE = FWD + 3 * CHUNKS
A_X = A_ONE + 8
A_CORE = A_X + 3
GA_CORE = A_CORE + 1
GA_X = GA_CORE + 1
GA_Z = GA_X + 3
W_CORE = GA_Z + 8
B_CORE = W_CORE + 1
W_XY = B_CORE + 1
W_Z1 = W_XY + 16
W_Z2 = W_Z1 + 3
W_AG = W_Z2 + 3
W_END = W_AG + 16
N_SEM = W_END + 1

CONTRACT_LANES = (((1,), (1,)), ((), ()))


def high(x):
    return x.astype(BF16).astype(F32)


def kernel(
    a_ref,
    b_ref,
    pg_ref,
    w_ref,
    ga_out,
    gb_out,
    gw_out,
    bias_out,
    g_all,
    a_all,
    ga_all,
    ga_r1,
    ga_r2,
    ga_s,
    ga_r3,
    gw_part,
    gw_r1,
    gw_s,
    gw_r2,
    gw_z1,
    gw_z2,
    bias_own,
    bias_r1,
    o_h,
    o_l,
    d_h,
    d_l,
    wp,
    bs,
    bo,
    bg,
    at,
    az,
    gp,
    acc_a,
    acc_w,
    bjs,
    send_sem,
    recv_sem,
):
    r = lax.axis_index("row")
    q = lax.axis_index("col")
    y = r // 2
    zh = r % 2
    zl = q // 8
    x = (q // 2) % 4
    core = q % 2
    z = zh * 8 + zl
    place = core * 4 + x
    xy = x * 4 + y

    def dev(y_, z_, x_, core_):
        return (y_ * 2 + z_ // 8, (z_ % 8) * 8 + x_ * 2 + core_)

    def rcopy(src, dst, number, device, arrives=None):
        return pltpu.make_async_remote_copy(
            src_ref=src,
            dst_ref=dst,
            send_sem=send_sem.at[number],
            recv_sem=recv_sem.at[number if arrives is None else arrives],
            device_id=device,
            device_id_type=MESH,
        )

    sibling = dev(y, z, x, 1 - core)
    twin = dev(y, (z + 8) % 16, x, core)
    y_peers = [dev((y + d) % 4, z, x, core) for d in (1, 2, 3)]
    x_peers = [dev(y, z, (x + d) % 4, core) for d in (1, 2, 3)]
    xy_steps = [(dx, dy) for dx in range(4) for dy in range(4) if (dx, dy) != (0, 0)]
    xy_peers = [dev((y + dy) % 4, z, (x + dx) % 4, core) for dx, dy in xy_steps]
    z_near = [dev(y, (z // 4) * 4 + (z + d) % 4, x, core) for d in (1, 2, 3)]
    z_far = [dev(y, (z + 4 * d) % 16, x, core) for d in (1, 2, 3)]
    out_a = [(zl, ((zl + d) % 8) * 8 + x * 2 + core) for d in range(8)]
    in_a = [((r + d) % 8, r * 8 + x * 2 + core) for d in range(8)]
    at_home = zl == r

    barrier = pltpu.get_barrier_semaphore()

    def greet(device):
        pl.semaphore_signal(barrier, inc=1, device_id=device, device_id_type=MESH)

    for device in out_a[1:] + in_a[1:] + z_far + z_near + xy_peers + [sibling]:
        greet(device)

    @pl.when(jnp.logical_not(at_home))
    def _():
        greet(out_a[0])
        greet(in_a[0])

    bias = jnp.zeros((8, K), F32)
    for j in range(32):
        block = pg_ref[pl.ds(j, 8, stride=32), :]
        g_all[r, j] = block
        bias = bias + block
    bias_own[...] = bias

    @pl.when(at_home)
    def _():
        a_all[place, r] = a_ref[...]

    fixed = 14 + 3 + 3 + 15 + 1
    pl.semaphore_wait(barrier, fixed + jnp.where(at_home, 0, 2))

    def chunk(m):
        return pl.ds(m * TC, TC)

    started = []

    def start(copy):
        copy.start()
        started.append(copy)
        return copy

    twin_copies = [
        rcopy(g_all.at[r, chunk(m)], g_all.at[r, chunk(m)], TWIN + m, twin) for m in range(CHUNKS)
    ]
    a_copies = [
        rcopy(a_ref, a_all.at[place, r], A_ONE + d, out_a[d], A_ONE + r) for d in range(8)
    ]
    a_waits = [
        rcopy(a_ref, a_all.at[place, r], A_ONE + d, out_a[d], A_ONE + (r + d) % 8)
        for d in range(8)
    ]

    @pl.when(jnp.logical_not(at_home))
    def _():
        a_copies[0].start()

    for d in range(1, 8):
        start(a_copies[d])
    for m in range(CHUNKS):
        start(twin_copies[m])
    own_copies = [start(rcopy(g_all.at[r], g_all.at[r], Y_OWN + n, y_peers[n])) for n in range(3)]

    low_lanes = lax.broadcasted_iota(jnp.int32, (32, 128), 1) < 64

    def split(v):
        h = v.astype(BF16)
        return h, (v - h.astype(F32)).astype(BF16)

    def prep_w(n, _):
        rows = pl.ds(pl.multiple_of(n * 128, 128), 128)
        h, l = split(w_ref[rows, :])
        wp[rows, 0:128] = h
        wp[rows, 128:256] = l
        wp[rows, 256:384] = h
        return 0

    lax.fori_loop(0, 8, prep_w, 0)

    for s in range(32):
        bs[s * 32 : (s + 1) * 32, 0:32] = b_ref[:, s * 32 : (s + 1) * 32]
    for jq in range(4):
        lanes = slice(jq * 128, (jq + 1) * 128)
        parts = []
        for jj in range(2):
            v = jnp.concatenate(
                [bs[pl.ds(8 * jq + 2 * t + jj, 32, stride=32), :][:, 0:32] for t in range(4)],
                axis=1,
            )
            h = high(v)
            parts.append((h, v - h))
            bg[jj * 32 : (jj + 1) * 32, lanes] = h.astype(BF16)
            bg[64 + jj * 32 : 64 + (jj + 1) * 32, lanes] = (v - h).astype(BF16)
        for n in range(2):
            v = jnp.concatenate([parts[0][n], parts[1][n]] * 2, axis=0)
            bo[lanes, n * 128 : (n + 1) * 128] = v.T.astype(BF16)

    forwards = {}

    def forward(m):
        twin_copies[m].wait_recv()
        for n in range(3):
            src = g_all.at[r + 1 - 2 * zh, chunk(m)]
            forwards[m, n] = start(rcopy(src, src, FWD + 3 * m + n, y_peers[n]))

    def prep_g(m):
        for n in range(3):
            forwards[2 * m, n].wait_recv()
            forwards[2 * m + 1, n].wait_recv()
        for j in range(m * JC, (m + 1) * JC):
            rows = slice(j * 64, (j + 1) * 64)
            gp[rows, 0:128], gp[rows, 128:256] = split(g_all[:, j].reshape(64, 128))

    def grad_outer(m):
        right = slice(m * JC * 64, (m + 1) * JC * 64)

        def make_d(n, _):
            for c2 in range(2):
                rows = pl.ds(pl.multiple_of(n * 256 + c2 * 128, 128), 128)
                v = lax.dot_general(
                    wp[rows, 0:256], gp[right, :], CONTRACT_LANES, preferred_element_type=F32
                ) + lax.dot_general(
                    wp[rows, 128:384], gp[right, :], CONTRACT_LANES, preferred_element_type=F32
                )
                h, l = split(v)
                for c in range(4):
                    lanes = pl.ds(pl.multiple_of(n * 1024 + (c2 * 4 + c) * 128, 128), 128)
                    for jp in range(4):
                        rows = slice((m * 4 + jp) * 32, (m * 4 + jp + 1) * 32)
                        part = (slice(c * 32, (c + 1) * 32), slice(jp * 128, (jp + 1) * 128))
                        d_h[rows, lanes] = h[part]
                        d_l[rows, lanes] = l[part]
            return 0

        lax.fori_loop(0, 4, make_d, 0)

    forward(0)
    for d in range(1, 8):
        a_waits[d].wait_recv()

    @pl.when(jnp.logical_not(at_home))
    def _():
        a_waits[0].wait_recv()

    ax_copies = [
        start(rcopy(a_all.at[place], a_all.at[place], A_X + n, x_peers[n])) for n in range(3)
    ]
    for m in range(1, 4):
        forward(m)
    for copy in ax_copies:
        copy.wait_recv()
    half = a_all.at[pl.ds(core * 4, 4)]
    ac_copy = start(rcopy(half, half, A_CORE, sibling))
    forward(4)
    for copy in own_copies:
        copy.wait_recv()
    prep_g(0)
    ac_copy.wait_recv()
    for core_ in range(2):
        for x_ in range(4):
            v = a_all[core_ * 4 + x_].reshape(64, 128)
            rows = slice((x_ * 2 + core_) * 128, (x_ * 2 + core_ + 1) * 128)
            at[rows, :] = jnp.concatenate([v, v], axis=0).T
    for c in range(32):
        v = at[pl.ds(c, 32, stride=32), :]
        h = high(v)
        l = v - h
        zero = jnp.zeros_like(v)
        v = jnp.concatenate(
            [
                jnp.where(low_lanes, h, zero),
                jnp.where(low_lanes, zero, h),
                jnp.where(low_lanes, l, zero),
                jnp.where(low_lanes, zero, l),
            ],
            axis=0,
        ).astype(BF16)
        lanes = slice(c * 128, (c + 1) * 128)
        az[0:128, lanes] = v
        az[128:256, lanes] = v
    forward(5)

    def make_o(n, _):
        right = az[:, pl.ds(pl.multiple_of(n * 256, 256), 256)]
        for jq in range(4):
            v = jnp.dot(bo[jq * 128 : (jq + 1) * 128, :], right, preferred_element_type=F32)
            h, l = split(v)
            for t in range(4):
                lanes = slice((jq * 4 + t) * 128, (jq * 4 + t + 1) * 128)
                for cc in range(2):
                    rows = pl.ds(pl.multiple_of(n * 64 + cc * 32, 32), 32)
                    part = (slice(t * 32, (t + 1) * 32), slice(cc * 128, (cc + 1) * 128))
                    o_h[rows, lanes] = h[part]
                    o_l[rows, lanes] = l[part]
        return 0

    lax.fori_loop(0, 8, make_o, 0)
    forward(6)
    lax.fori_loop(8, 16, make_o, 0)
    forward(7)

    for m in range(4):
        if m:
            prep_g(m)

        def add_w(n, _):
            rows = pl.ds(pl.multiple_of(n * 256, 256), 256)
            lanes = slice(m * 512, (m + 1) * 512)
            right = gp[m * 512 : (m + 1) * 512, :]
            v = jnp.dot(o_h[rows, lanes], right, preferred_element_type=F32) + jnp.dot(
                o_l[rows, lanes], right, preferred_element_type=F32
            )
            if m:
                v = v + acc_w[rows, :]
            if m < 3:
                acc_w[rows, :] = v
            else:
                gw_part[rows, :] = (v[:, 0:128] + v[:, 128:256]) * (1.0 / S)
            return 0

        lax.fori_loop(0, 4, add_w, 0)

    other = pl.ds(pl.multiple_of((1 - core) * 512, 512), 512)
    w_core = start(rcopy(gw_part.at[other], gw_r1, W_CORE, sibling))
    b_core = start(rcopy(bias_own, bias_r1, B_CORE, sibling))

    grad_outer(0)
    w_core.wait_recv()
    b_core.wait_recv()
    bias = bias_own[...] + bias_r1[...]

    def add_core(n, _):
        rows = pl.ds(pl.multiple_of(n * 32, 32), 32)
        mine = pl.ds(pl.multiple_of(core * 512 + n * 32, 32), 32)
        gw_s[n, 0:32] = gw_part[mine, :] + gw_r1[rows, :]
        gw_s[n, 32:40] = bias
        return 0

    lax.fori_loop(0, 16, add_core, 0)
    gw_r2[xy] = gw_s[xy]
    w_xy = []
    for n, (dx, dy) in enumerate(xy_steps):
        to = ((x + dx) % 4) * 4 + (y + dy) % 4
        w_xy.append(start(rcopy(gw_s.at[to], gw_r2.at[xy], W_XY + n, xy_peers[n])))

    def add_b(m):
        rows = slice(m * 128, (m + 1) * 128)
        v = jnp.zeros((128, 128), F32)
        for n in range(4):
            lanes = slice(n * 1024, (n + 1) * 1024)
            v = v + lax.dot_general(
                d_h[rows, lanes], az[0:128, lanes], CONTRACT_LANES, preferred_element_type=F32
            )
            v = v + lax.dot_general(
                d_l[rows, lanes], az[0:128, lanes], CONTRACT_LANES, preferred_element_type=F32
            )
        v = v.T
        v = (v[0:64] + v[64:128]) * (1.0 / S)
        for t in range(4):
            jp = m * 4 + t
            bjs[jp * 64 : (jp + 1) * 64, 0:32] = v[:, t * 32 : (t + 1) * 32]

    for m in range(1, 4):
        grad_outer(m)
    for copy in w_xy:
        copy.wait_recv()
    v = gw_r2[0]
    for n in range(1, 16):
        v = v + gw_r2[n]
    gw_z1[z % 4] = v
    w_z1 = [
        start(rcopy(gw_z1.at[z % 4], gw_z1.at[z % 4], W_Z1 + n, z_near[n])) for n in range(3)
    ]
    def add_a(n, _):
        lanes = pl.ds(pl.multiple_of(n * 256, 256), 256)
        v = jnp.dot(bg[...], d_h[:, lanes], preferred_element_type=F32) + jnp.dot(
            bg[...], d_l[:, lanes], preferred_element_type=F32
        )
        v = v[0:64] + v[64:128]
        for cc in range(2):
            part = v[:, cc * 128 : (cc + 1) * 128]
            rows = pl.ds(pl.multiple_of(n * 64 + cc * 32, 32), 32)
            acc_a[rows, :] = jnp.where(low_lanes, part[0:32], part[32:64])
        return 0

    lax.fori_loop(0, 16, add_a, 0)
    for core_ in range(2):
        for x_ in range(4):
            s0 = 4 * (x_ * 2 + core_)
            v = jnp.concatenate(
                [acc_a[pl.ds(s0 + s, 32, stride=32), :] for s in range(4)], axis=0
            ).T
            ga_all[core_, x_] = ((v[0:64] + v[64:128]) * (1.0 / S)).reshape(8, 8, 128)
    ga_core = start(rcopy(ga_all.at[1 - core], ga_r1, GA_CORE, sibling))

    for copy in w_z1:
        copy.wait_recv()
    gw_z2[z // 4] = (gw_z1[0] + gw_z1[1]) + (gw_z1[2] + gw_z1[3])
    w_z2 = [
        start(rcopy(gw_z2.at[z // 4], gw_z2.at[z // 4], W_Z2 + n, z_far[n])) for n in range(3)
    ]
    ga_core.wait_recv()
    for x_ in range(4):
        ga_r1[x_] = ga_r1[x_] + ga_all[core, x_]
    ga_r2[x] = ga_r1[x]
    ga_x = []
    for n, d in enumerate((1, 2, 3)):
        ga_x.append(start(rcopy(ga_r1.at[(x + d) % 4], ga_r2.at[x], GA_X + n, x_peers[n])))

    add_b(0)
    add_b(1)
    for copy in ga_x:
        copy.wait_recv()
    ga_s[...] = (ga_r2[0] + ga_r2[1]) + (ga_r2[2] + ga_r2[3])
    ga_z = [
        rcopy(ga_s.at[(r + d) % 8], ga_r3.at[zl], GA_Z + d, in_a[d], GA_Z + zl) for d in range(8)
    ]
    ga_waits = [
        rcopy(ga_s.at[d], ga_r3.at[zl], GA_Z + d, in_a[d], GA_Z + (zl + d) % 8) for d in range(8)
    ]

    @pl.when(jnp.logical_not(at_home))
    def _():
        ga_z[0].start()

    @pl.when(at_home)
    def _():
        ga_r3[zl] = ga_s[r]

    for d in range(1, 8):
        start(ga_z[d])
    for copy in w_z2:
        copy.wait_recv()
    v = (gw_z2[0] + gw_z2[1]) + (gw_z2[2] + gw_z2[3])
    mine = pl.ds(pl.multiple_of(core * 512 + xy * 32, 32), 32)
    gw_out[mine, :] = v[0:32]
    w_ag = [
        start(rcopy(gw_out.at[mine], gw_out.at[mine], W_AG + n, xy_peers[n])) for n in range(15)
    ]
    bias_out[...] = jnp.sum(v[32:40], axis=0, keepdims=True)
    add_b(2)
    add_b(3)
    for s in range(32):
        gb_out[:, s * 32 : (s + 1) * 32] = bjs[pl.ds(s, 32, stride=32), :][:, 0:32]
    for copy in w_ag:
        copy.wait_recv()
    mine = gw_out.at[pl.ds(pl.multiple_of(core * 512, 512), 512)]
    w_end = start(rcopy(mine, mine, W_END, sibling))
    for d in range(1, 8):
        ga_waits[d].wait_recv()

    @pl.when(jnp.logical_not(at_home))
    def _():
        ga_waits[0].wait_recv()

    v = ga_r3[0]
    for n in range(1, 8):
        v = v + ga_r3[n]
    ga_out[...] = v
    w_end.wait_recv()
    for copy in started:
        copy.wait_send()

    @pl.when(jnp.logical_not(at_home))
    def _():
        a_copies[0].wait_send()
        ga_z[0].wait_send()


def hand_over(*refs):
    for n in range(4):
        refs[4 + n][...] = refs[n][...]


def local(side_a, side_b, pair_grad, out_weight):
    vmem = pl.BlockSpec(memory_space=pltpu.VMEM)
    flat = pair_grad.reshape(256, K)
    ga, gb, gw, bias = pl.pallas_call(
        kernel,
        out_shape=(
            jax.ShapeDtypeStruct((8, 128), F32),
            jax.ShapeDtypeStruct((32, 1024), F32),
            jax.ShapeDtypeStruct((1024, 128), F32),
            jax.ShapeDtypeStruct((1, 128), F32),
        ),
        in_specs=[vmem] * 4,
        out_specs=(vmem,) * 4,
        scratch_shapes=[
            pltpu.VMEM((8, 32, 8, 128), F32),
            pltpu.VMEM((8, 8, 8, 128), F32),
            pltpu.VMEM((2, 4, 8, 8, 128), F32),
            pltpu.VMEM((4, 8, 8, 128), F32),
            pltpu.VMEM((4, 8, 8, 128), F32),
            pltpu.VMEM((8, 8, 128), F32),
            pltpu.VMEM((8, 8, 128), F32),
            pltpu.VMEM((1024, 128), F32),
            pltpu.VMEM((512, 128), F32),
            pltpu.VMEM((16, 40, 128), F32),
            pltpu.VMEM((16, 40, 128), F32),
            pltpu.VMEM((4, 40, 128), F32),
            pltpu.VMEM((4, 40, 128), F32),
            pltpu.VMEM((8, 128), F32),
            pltpu.VMEM((8, 128), F32),
            pltpu.VMEM((1024, 2048), BF16),
            pltpu.VMEM((1024, 2048), BF16),
            pltpu.VMEM((512, 4096), BF16),
            pltpu.VMEM((512, 4096), BF16),
            pltpu.VMEM((1024, 384), BF16),
            pltpu.VMEM((1024, 128), F32),
            pltpu.VMEM((512, 256), BF16),
            pltpu.VMEM((128, 512), BF16),
            pltpu.VMEM((1024, 128), F32),
            pltpu.VMEM((256, 4096), BF16),
            pltpu.VMEM((2048, 256), BF16),
            pltpu.VMEM((1024, 128), F32),
            pltpu.VMEM((1024, 256), F32),
            pltpu.VMEM((1024, 128), F32),
            pltpu.SemaphoreType.DMA((N_SEM,)),
            pltpu.SemaphoreType.DMA((N_SEM,)),
        ],
        compiler_params=pltpu.CompilerParams(
            collective_id=0, has_side_effects=True, vmem_limit_bytes=60 * 1024 * 1024
        ),
    )(side_a, side_b, flat, out_weight)
    arrays = (ga, gb, gw, bias)
    ga, gb, gw, bias = pl.pallas_call(
        hand_over,
        out_shape=tuple(jax.ShapeDtypeStruct(v.shape, v.dtype) for v in arrays),
        in_specs=[vmem] * 4,
        out_specs=(vmem,) * 4,
    )(*arrays)
    return ga, gb, gw, bias.reshape(K)


def solution(mesh):
    in_specs = (P("row", "col"), P("col", "row"), P("row", "col", None), P())
    out_specs = (P("row", "col"), P("col", "row"), P(), P())
    return jax.shard_map(local, mesh=mesh, in_specs=in_specs, out_specs=out_specs, check_vma=False)
```

```python
import jax
import jax.numpy as jnp
from jax import lax
from jax.experimental import pallas as pl
from jax.experimental.pallas import tpu as pltpu
from jax.sharding import PartitionSpec as P

S = 256
C = 32
K = 128
CHUNKS = 8
TC = 32 // CHUNKS
JC = 8
MESH = pl.DeviceIdType.MESH
F32 = jnp.float32
BF16 = jnp.bfloat16

Y_OWN = 0
TWIN = Y_OWN + 3
FWD = TWIN + CHUNKS
A_ONE = FWD + 3 * CHUNKS
A_X = A_ONE + 8
A_CORE = A_X + 3
GA_CORE = A_CORE + 1
GA_X = GA_CORE + 1
GA_Z = GA_X + 3
W_CORE = GA_Z + 8
B_CORE = W_CORE + 1
W_XY = B_CORE + 1
W_Z1 = W_XY + 16
W_Z2 = W_Z1 + 3
W_AG = W_Z2 + 3
W_END = W_AG + 16
N_SEM = W_END + 16

CONTRACT_LANES = (((1,), (1,)), ((), ()))


def high(x):
    return x.astype(BF16).astype(F32)


def kernel(
    a_ref,
    b_ref,
    pg_ref,
    w_ref,
    ga_out,
    gb_out,
    gw_out,
    bias_out,
    g_all,
    a_all,
    ga_all,
    ga_r1,
    ga_r2,
    ga_s,
    ga_r3,
    gw_part,
    gw_r1,
    gw_s,
    gw_r2,
    gw_z1,
    gw_z2,
    bias_own,
    bias_r1,
    o_h,
    o_l,
    d_h,
    d_l,
    wp,
    bs,
    bo,
    bg,
    at,
    az,
    gp,
    gt,
    acc_a,
    acc_w,
    bjs,
    send_sem,
    recv_sem,
):
    r = lax.axis_index("row")
    q = lax.axis_index("col")
    y = r // 2
    zh = r % 2
    zl = q // 8
    x = (q // 2) % 4
    core = q % 2
    z = zh * 8 + zl
    place = core * 4 + x
    xy = x * 4 + y

    def dev(y_, z_, x_, core_):
        return (y_ * 2 + z_ // 8, (z_ % 8) * 8 + x_ * 2 + core_)

    def rcopy(src, dst, number, device, arrives=None):
        return pltpu.make_async_remote_copy(
            src_ref=src,
            dst_ref=dst,
            send_sem=send_sem.at[number],
            recv_sem=recv_sem.at[number if arrives is None else arrives],
            device_id=device,
            device_id_type=MESH,
        )

    sibling = dev(y, z, x, 1 - core)
    twin = dev(y, (z + 8) % 16, x, core)
    y_peers = [dev((y + d) % 4, z, x, core) for d in (1, 2, 3)]
    x_peers = [dev(y, z, (x + d) % 4, core) for d in (1, 2, 3)]
    xy_steps = [(dx, dy) for dx in (2, 1, 3, 0) for dy in (2, 1, 3, 0) if (dx, dy) != (0, 0)]
    xy_steps.sort(key=lambda step: sum(min(d, 4 - d) for d in step), reverse=True)
    xy_peers = [dev((y + dy) % 4, z, (x + dx) % 4, core) for dx, dy in xy_steps]
    z_near = [dev(y, (z // 4) * 4 + (z + d) % 4, x, core) for d in (1, 2, 3)]
    z_far = [dev(y, (z + 4 * d) % 16, x, core) for d in (2, 1, 3)]
    out_a = [(zl, ((zl + d) % 8) * 8 + x * 2 + core) for d in range(8)]
    in_a = [((r + d) % 8, r * 8 + x * 2 + core) for d in range(8)]
    at_home = zl == r

    barrier = pltpu.get_barrier_semaphore()

    def greet(device):
        pl.semaphore_signal(barrier, inc=1, device_id=device, device_id_type=MESH)

    for device in out_a[1:] + in_a[1:] + z_far + z_near + xy_peers + [sibling]:
        greet(device)

    @pl.when(jnp.logical_not(at_home))
    def _():
        greet(out_a[0])
        greet(in_a[0])

    bias = jnp.zeros((8, K), F32)
    for j in range(32):
        block = pg_ref[pl.ds(j, 8, stride=32), :]
        g_all[r, j] = block
        bias = bias + block
    bias_own[...] = bias

    @pl.when(at_home)
    def _():
        a_all[place, r] = a_ref[...]

    fixed = 14 + 3 + 3 + 15 + 1
    pl.semaphore_wait(barrier, fixed + jnp.where(at_home, 0, 2))

    def chunk(m):
        return pl.ds(m * TC, TC)

    started = []

    def start(copy):
        copy.start()
        started.append(copy)
        return copy

    twin_copies = [
        rcopy(g_all.at[r, chunk(m)], g_all.at[r, chunk(m)], TWIN + m, twin) for m in range(CHUNKS)
    ]
    a_copies = [
        rcopy(a_ref, a_all.at[place, r], A_ONE + d, out_a[d], A_ONE + r) for d in range(8)
    ]
    a_waits = [
        rcopy(a_ref, a_all.at[place, r], A_ONE + d, out_a[d], A_ONE + (r + d) % 8)
        for d in range(8)
    ]

    @pl.when(jnp.logical_not(at_home))
    def _():
        a_copies[0].start()

    for d in range(1, 8):
        start(a_copies[d])
    for m in range(CHUNKS):
        start(twin_copies[m])
    own_copies = [start(rcopy(g_all.at[r], g_all.at[r], Y_OWN + n, y_peers[n])) for n in range(3)]

    low_lanes = lax.broadcasted_iota(jnp.int32, (32, 128), 1) < 64

    def split(v):
        h = v.astype(BF16)
        return h, (v - h.astype(F32)).astype(BF16)

    def prep_w(n, _):
        rows = pl.ds(pl.multiple_of(n * 128, 128), 128)
        h, l = split(w_ref[rows, :])
        wp[rows, 0:128] = h
        wp[rows, 128:256] = l
        wp[rows, 256:384] = h
        return 0

    lax.fori_loop(0, 8, prep_w, 0)

    for s in range(32):
        bs[s * 32 : (s + 1) * 32, 0:32] = b_ref[:, s * 32 : (s + 1) * 32]
    for jq in range(4):
        lanes = slice(jq * 128, (jq + 1) * 128)
        parts = []
        for jj in range(2):
            v = jnp.concatenate(
                [bs[pl.ds(8 * jq + 2 * t + jj, 32, stride=32), :][:, 0:32] for t in range(4)],
                axis=1,
            )
            h = high(v)
            parts.append((h, v - h))
            bg[jj * 32 : (jj + 1) * 32, lanes] = h.astype(BF16)
            bg[64 + jj * 32 : 64 + (jj + 1) * 32, lanes] = (v - h).astype(BF16)
        for n in range(2):
            v = jnp.concatenate([parts[0][n], parts[1][n]] * 2, axis=0)
            bo[lanes, n * 128 : (n + 1) * 128] = v.T.astype(BF16)

    forwards = {}

    def forward(m):
        twin_copies[m].wait_recv()
        for n in range(3):
            src = g_all.at[r + 1 - 2 * zh, chunk(m)]
            forwards[m, n] = start(rcopy(src, src, FWD + 3 * m + n, y_peers[n]))

    def prep_g(m):
        for n in range(3):
            forwards[2 * m, n].wait_recv()
            forwards[2 * m + 1, n].wait_recv()
        for jp in range(m * JC // 2, (m + 1) * JC // 2):
            v = jnp.concatenate(
                [g_all[:, 2 * jp].reshape(64, 128), g_all[:, 2 * jp + 1].reshape(64, 128)], axis=0
            )
            rows = slice(jp * 128, (jp + 1) * 128)
            gp[rows, 0:128], gp[rows, 128:256] = split(v)
            gt[0:128, rows], gt[128:256, rows] = split(v.T)

    def grad_outer(m):
        right = slice(m * JC * 64, (m + 1) * JC * 64)

        def make_d(n, _):
            for c2 in range(2):
                rows = pl.ds(pl.multiple_of(n * 256 + c2 * 128, 128), 128)
                v = jnp.dot(
                    wp[rows, 0:256], gt[:, right], preferred_element_type=F32
                ) + jnp.dot(wp[rows, 128:384], gt[:, right], preferred_element_type=F32)
                h, l = split(v)
                for c in range(4):
                    lanes = pl.ds(pl.multiple_of(n * 1024 + (c2 * 4 + c) * 128, 128), 128)
                    for jp in range(4):
                        rows = slice((m * 4 + jp) * 32, (m * 4 + jp + 1) * 32)
                        part = (slice(c * 32, (c + 1) * 32), slice(jp * 128, (jp + 1) * 128))
                        d_h[rows, lanes] = h[part]
                        d_l[rows, lanes] = l[part]
            return 0

        lax.fori_loop(0, 4, make_d, 0)

    forward(0)
    for d in range(1, 8):
        a_waits[d].wait_recv()

    @pl.when(jnp.logical_not(at_home))
    def _():
        a_waits[0].wait_recv()

    ax_copies = [
        start(rcopy(a_all.at[place], a_all.at[place], A_X + n, x_peers[n])) for n in range(3)
    ]
    for m in range(1, 4):
        forward(m)
    for copy in ax_copies:
        copy.wait_recv()
    half = a_all.at[pl.ds(core * 4, 4)]
    ac_copy = start(rcopy(half, half, A_CORE, sibling))
    forward(4)
    for copy in own_copies:
        copy.wait_recv()
    prep_g(0)
    ac_copy.wait_recv()
    for core_ in range(2):
        for x_ in range(4):
            v = a_all[core_ * 4 + x_].reshape(64, 128)
            rows = slice((x_ * 2 + core_) * 128, (x_ * 2 + core_ + 1) * 128)
            at[rows, :] = jnp.concatenate([v, v], axis=0).T
    for c in range(32):
        v = at[pl.ds(c, 32, stride=32), :]
        h = high(v)
        l = v - h
        zero = jnp.zeros_like(v)
        v = jnp.concatenate(
            [
                jnp.where(low_lanes, h, zero),
                jnp.where(low_lanes, zero, h),
                jnp.where(low_lanes, l, zero),
                jnp.where(low_lanes, zero, l),
            ],
            axis=0,
        ).astype(BF16)
        lanes = slice(c * 128, (c + 1) * 128)
        az[0:128, lanes] = v
        az[128:256, lanes] = v
    forward(5)

    def make_o(n, _):
        right = az[:, pl.ds(pl.multiple_of(n * 256, 256), 256)]
        for jq in range(4):
            v = jnp.dot(bo[jq * 128 : (jq + 1) * 128, :], right, preferred_element_type=F32)
            h, l = split(v)
            for t in range(4):
                lanes = slice((jq * 4 + t) * 128, (jq * 4 + t + 1) * 128)
                for cc in range(2):
                    rows = pl.ds(pl.multiple_of(n * 64 + cc * 32, 32), 32)
                    part = (slice(t * 32, (t + 1) * 32), slice(cc * 128, (cc + 1) * 128))
                    o_h[rows, lanes] = h[part]
                    o_l[rows, lanes] = l[part]
        return 0

    lax.fori_loop(0, 8, make_o, 0)
    forward(6)
    lax.fori_loop(8, 16, make_o, 0)
    forward(7)

    for m in range(1, 4):
        prep_g(m)

    def add_w(first):
        def step(n, _):
            rows = pl.ds(pl.multiple_of(first + n * 256, 256), 256)
            gw = jnp.dot(o_h[rows, :], gp[...], preferred_element_type=F32) + jnp.dot(
                o_l[rows, :], gp[...], preferred_element_type=F32
            )
            gw_part[rows, :] = (gw[:, 0:128] + gw[:, 128:256]) * (1.0 / S)
            return 0

        lax.fori_loop(0, 2, step, 0)

    b_core = start(rcopy(bias_own, bias_r1, B_CORE, sibling))
    add_w((1 - core) * 512)
    other = pl.ds(pl.multiple_of((1 - core) * 512, 512), 512)
    w_core = start(rcopy(gw_part.at[other], gw_r1, W_CORE, sibling))
    add_w(core * 512)
    w_core.wait_recv()
    b_core.wait_recv()
    bias = bias_own[...] + bias_r1[...]

    def add_core(n, _):
        rows = pl.ds(pl.multiple_of(n * 32, 32), 32)
        mine = pl.ds(pl.multiple_of(core * 512 + n * 32, 32), 32)
        gw_s[n, 0:32] = gw_part[mine, :] + gw_r1[rows, :]
        gw_s[n, 32:40] = bias
        return 0

    lax.fori_loop(0, 16, add_core, 0)
    gw_r2[xy] = gw_s[xy]
    w_xy = []
    for n, (dx, dy) in enumerate(xy_steps):
        to = ((x + dx) % 4) * 4 + (y + dy) % 4
        w_xy.append(start(rcopy(gw_s.at[to], gw_r2.at[xy], W_XY + n, xy_peers[n])))

    def add_b(m):
        rows = slice(m * 128, (m + 1) * 128)
        v = jnp.zeros((128, 128), F32)
        for n in range(4):
            lanes = slice(n * 1024, (n + 1) * 1024)
            v = v + lax.dot_general(
                d_h[rows, lanes], az[0:128, lanes], CONTRACT_LANES, preferred_element_type=F32
            )
            v = v + lax.dot_general(
                d_l[rows, lanes], az[0:128, lanes], CONTRACT_LANES, preferred_element_type=F32
            )
        v = v.T
        v = (v[0:64] + v[64:128]) * (1.0 / S)
        for t in range(4):
            jp = m * 4 + t
            bjs[jp * 64 : (jp + 1) * 64, 0:32] = v[:, t * 32 : (t + 1) * 32]

    for m in range(4):
        grad_outer(m)
    def add_a(n, _):
        lanes = pl.ds(pl.multiple_of(n * 256, 256), 256)
        v = jnp.dot(bg[...], d_h[:, lanes], preferred_element_type=F32) + jnp.dot(
            bg[...], d_l[:, lanes], preferred_element_type=F32
        )
        v = v[0:64] + v[64:128]
        for cc in range(2):
            part = v[:, cc * 128 : (cc + 1) * 128]
            rows = pl.ds(pl.multiple_of(n * 64 + cc * 32, 32), 32)
            acc_a[rows, :] = jnp.where(low_lanes, part[0:32], part[32:64])
        return 0

    lax.fori_loop(0, 10, add_a, 0)
    for copy in w_xy:
        copy.wait_recv()
    v = gw_r2[0]
    for n in range(1, 16):
        v = v + gw_r2[n]
    gw_z1[z % 4] = v
    w_z1 = [
        start(rcopy(gw_z1.at[z % 4], gw_z1.at[z % 4], W_Z1 + n, z_near[n])) for n in range(3)
    ]
    lax.fori_loop(10, 16, add_a, 0)
    for core_ in range(2):
        for x_ in range(4):
            s0 = 4 * (x_ * 2 + core_)
            v = jnp.concatenate(
                [acc_a[pl.ds(s0 + s, 32, stride=32), :] for s in range(4)], axis=0
            ).T
            ga_all[core_, x_] = ((v[0:64] + v[64:128]) * (1.0 / S)).reshape(8, 8, 128)
    ga_core = start(rcopy(ga_all.at[1 - core], ga_r1, GA_CORE, sibling))

    ga_core.wait_recv()
    for x_ in range(4):
        ga_r1[x_] = ga_r1[x_] + ga_all[core, x_]
    ga_r2[x] = ga_r1[x]
    ga_x = []
    for n, d in enumerate((1, 2, 3)):
        ga_x.append(start(rcopy(ga_r1.at[(x + d) % 4], ga_r2.at[x], GA_X + n, x_peers[n])))

    for copy in w_z1:
        copy.wait_recv()
    gw_z2[z // 4] = (gw_z1[0] + gw_z1[1]) + (gw_z1[2] + gw_z1[3])
    w_z2 = [
        start(rcopy(gw_z2.at[z // 4], gw_z2.at[z // 4], W_Z2 + n, z_far[n])) for n in range(3)
    ]
    for copy in ga_x:
        copy.wait_recv()
    ga_s[...] = (ga_r2[0] + ga_r2[1]) + (ga_r2[2] + ga_r2[3])
    ga_z = [
        rcopy(ga_s.at[(r + d) % 8], ga_r3.at[zl], GA_Z + d, in_a[d], GA_Z + zl) for d in range(8)
    ]
    ga_waits = [
        rcopy(ga_s.at[d], ga_r3.at[zl], GA_Z + d, in_a[d], GA_Z + (zl + d) % 8) for d in range(8)
    ]

    @pl.when(jnp.logical_not(at_home))
    def _():
        ga_z[0].start()

    @pl.when(at_home)
    def _():
        ga_r3[zl] = ga_s[r]

    for d in range(1, 8):
        start(ga_z[d])
    add_b(0)
    add_b(1)
    for copy in w_z2:
        copy.wait_recv()
    v = (gw_z2[0] + gw_z2[1]) + (gw_z2[2] + gw_z2[3])
    mine = pl.ds(pl.multiple_of(core * 512 + xy * 32, 32), 32)
    gw_out[mine, :] = v[0:32]
    w_ag = [
        start(rcopy(gw_out.at[mine], gw_out.at[mine], W_AG + n, xy_peers[n])) for n in range(15)
    ]
    w_end = [start(rcopy(gw_out.at[mine], gw_out.at[mine], W_END + 15, sibling))]
    bias_out[...] = jnp.sum(v[32:40], axis=0, keepdims=True)
    add_b(2)
    add_b(3)
    for s in range(32):
        gb_out[:, s * 32 : (s + 1) * 32] = bjs[pl.ds(s, 32, stride=32), :][:, 0:32]
    for n in reversed(range(15)):
        w_ag[n].wait_recv()
        dx, dy = xy_steps[n]
        from_xy = ((x - dx) % 4) * 4 + (y - dy) % 4
        part = gw_out.at[pl.ds(pl.multiple_of(core * 512 + from_xy * 32, 32), 32)]
        w_end.append(start(rcopy(part, part, W_END + n, sibling)))
    for d in range(1, 8):
        ga_waits[d].wait_recv()

    @pl.when(jnp.logical_not(at_home))
    def _():
        ga_waits[0].wait_recv()

    v = ga_r3[0]
    for n in range(1, 8):
        v = v + ga_r3[n]
    ga_out[...] = v
    for copy in w_end:
        copy.wait_recv()
    for copy in started:
        copy.wait_send()

    @pl.when(jnp.logical_not(at_home))
    def _():
        a_copies[0].wait_send()
        ga_z[0].wait_send()


def hand_over(*refs):
    for n in range(4):
        refs[4 + n][...] = refs[n][...]


def local(side_a, side_b, pair_grad, out_weight):
    vmem = pl.BlockSpec(memory_space=pltpu.VMEM)
    flat = pair_grad.reshape(256, K)
    ga, gb, gw, bias = pl.pallas_call(
        kernel,
        out_shape=(
            jax.ShapeDtypeStruct((8, 128), F32),
            jax.ShapeDtypeStruct((32, 1024), F32),
            jax.ShapeDtypeStruct((1024, 128), F32),
            jax.ShapeDtypeStruct((1, 128), F32),
        ),
        in_specs=[vmem] * 4,
        out_specs=(vmem,) * 4,
        scratch_shapes=[
            pltpu.VMEM((8, 32, 8, 128), F32),
            pltpu.VMEM((8, 8, 8, 128), F32),
            pltpu.VMEM((2, 4, 8, 8, 128), F32),
            pltpu.VMEM((4, 8, 8, 128), F32),
            pltpu.VMEM((4, 8, 8, 128), F32),
            pltpu.VMEM((8, 8, 128), F32),
            pltpu.VMEM((8, 8, 128), F32),
            pltpu.VMEM((1024, 128), F32),
            pltpu.VMEM((512, 128), F32),
            pltpu.VMEM((16, 40, 128), F32),
            pltpu.VMEM((16, 40, 128), F32),
            pltpu.VMEM((4, 40, 128), F32),
            pltpu.VMEM((4, 40, 128), F32),
            pltpu.VMEM((8, 128), F32),
            pltpu.VMEM((8, 128), F32),
            pltpu.VMEM((1024, 2048), BF16),
            pltpu.VMEM((1024, 2048), BF16),
            pltpu.VMEM((512, 4096), BF16),
            pltpu.VMEM((512, 4096), BF16),
            pltpu.VMEM((1024, 384), BF16),
            pltpu.VMEM((1024, 128), F32),
            pltpu.VMEM((512, 256), BF16),
            pltpu.VMEM((128, 512), BF16),
            pltpu.VMEM((1024, 128), F32),
            pltpu.VMEM((256, 4096), BF16),
            pltpu.VMEM((2048, 256), BF16),
            pltpu.VMEM((256, 2048), BF16),
            pltpu.VMEM((1024, 128), F32),
            pltpu.VMEM((1024, 256), F32),
            pltpu.VMEM((1024, 128), F32),
            pltpu.SemaphoreType.DMA((N_SEM,)),
            pltpu.SemaphoreType.DMA((N_SEM,)),
        ],
        compiler_params=pltpu.CompilerParams(
            collective_id=0, has_side_effects=True, vmem_limit_bytes=60 * 1024 * 1024
        ),
    )(side_a, side_b, flat, out_weight)
    arrays = (ga, gb, gw, bias)
    ga, gb, gw, bias = pl.pallas_call(
        hand_over,
        out_shape=tuple(jax.ShapeDtypeStruct(v.shape, v.dtype) for v in arrays),
        in_specs=[vmem] * 4,
        out_specs=(vmem,) * 4,
    )(*arrays)
    return ga, gb, gw, bias.reshape(K)


def solution(mesh):
    in_specs = (P("row", "col"), P("col", "row"), P("row", "col", None), P())
    out_specs = (P("row", "col"), P("col", "row"), P(), P())
    return jax.shard_map(local, mesh=mesh, in_specs=in_specs, out_specs=out_specs, check_vma=False)
```
